32 devices in a mesh: seq: 8 (over y, x, core), head: 4 (over z).
Axes of the slice: x: 2, y: 2, z: 4, core: 2. Of those that a mesh axis runs over, the one named last changes fastest.
Arguments:
- tokens: bfloat16 [16384, 640], P(('seq', 'head')), may hold values from -6 to 6
- positions: int32 [16384], P('seq'), may hold values from 0 to 16383, as said below
- w_query: bfloat16 [640, 1024], P('seq'), may hold values from -0.25 to 0.25
- w_key: bfloat16 [640, 256], P('seq'), may hold values from -0.25 to 0.25
- w_value: bfloat16 [640, 256], P('seq'), may hold values from -0.25 to 0.25
- w_out: bfloat16 [1024, 640], P(None, 'seq'), may hold values from -0.1875 to 0.1875
- w_gate: bfloat16 [640, 2048], P('seq'), may hold values from -0.25 to 0.25
- w_up: bfloat16 [640, 2048], P('seq'), may hold values from -0.25 to 0.25
- w_down: bfloat16 [2048, 640], P(None, 'seq'), may hold values from -0.125 to 0.125
- gain_input: bfloat16 [640], P('seq'), may hold values from -0.5 to 0.5
- gain_attn: bfloat16 [640], P('seq'), may hold values from -0.5 to 0.5
- gain_ffn_in: bfloat16 [640], P('seq'), may hold values from -0.5 to 0.5
- gain_ffn_out: bfloat16 [640], P('seq'), may hold values from -0.5 to 0.5
- gain_query: bfloat16 [256], P('seq'), may hold values from -0.5 to 0.5
- gain_key: bfloat16 [256], P('seq'), may hold values from -0.5 to 0.5
- cotangent: bfloat16 [16384, 640], P(('seq', 'head')), may hold values from -6 to 6
Outputs:
- block_out: bfloat16 [16384, 640], P(('seq', 'head'))
- grad_tokens: float32 [16384, 640], P(('seq', 'head'))
- grad_w_query: float32 [640, 1024], P('seq')
- grad_w_key: float32 [640, 256], P('seq')
- grad_w_value: float32 [640, 256], P('seq')
- grad_w_out: float32 [1024, 640], P(None, 'seq')
- grad_w_gate: float32 [640, 2048], P('seq')
- grad_w_up: float32 [640, 2048], P('seq')
- grad_w_down: float32 [2048, 640], P(None, 'seq')
- grad_gain_input: float32 [640], P('seq')
- grad_gain_attn: float32 [640], P('seq')
- grad_gain_ffn_in: float32 [640], P('seq')
- grad_gain_ffn_out: float32 [640], P('seq')
- grad_gain_query: float32 [256], P('seq')
- grad_gain_key: float32 [256], P('seq')
The draws below stay inside these ranges and needn't reach their ends.
Inputs may be any that keep to these rules, and one draw needn't show every extreme that they name: There are three sequences. Within a sequence positions rise by one from token to token. The first sequence starts at token 0 and ends within the last 2048 tokens, where its position is 16383; the two later sequences start at position 0.
All inputs are finite; a program needn't handle non-finite values.
Results may differ from the reference program's by a relative error of at most 0.02.
Values may be sent and summed in bfloat16 or wider, within the bound.
A program may use at most 128 MiB of HBM per device.

```python
import math
import jax
import jax.numpy as jnp
from jax import lax

D = 640
HD = 256
FF = 2048
WINDOW = 512
QBLOCK = 512
HEADS = 4
GROUP = 2048
TOKENS = 16384


def draw_positions(key, part):
    key = jax.random.fold_in(key, 7)
    tail_key, split_key = jax.random.split(key)
    tail_len = jax.random.randint(tail_key, (), 2, GROUP)
    first_len = TOKENS - tail_len
    second_len = jax.random.randint(split_key, (), 1, tail_len)
    token_index = jnp.arange(TOKENS, dtype=jnp.int32)
    later = jnp.where(token_index < first_len + second_len, token_index - first_len, token_index - first_len - second_len)
    return jnp.where(token_index < first_len, token_index + tail_len, later).astype(jnp.int32)


def raised(result, rng, source, target, blocks, factor):
    owner, partner = [(jnp.arange(result.shape[dim]) // (result.shape[dim] // blocks)).reshape([-1 if axis == dim else 1 for axis in range(result.ndim)]) for dim in (source, target)]
    chosen = jax.random.permutation(rng, blocks)[partner]
    strong = (owner == chosen) | (owner == (partner + blocks // 2) % blocks)
    return jnp.where(strong, factor * result, result)


def block_scale(own_key, shape, pieces, smallest, high):
    loudness = 1.0
    for position, parts in pieces:
        draws = jax.random.uniform(jax.random.fold_in(jax.random.fold_in(own_key, 6), position), (parts,), jnp.float32, smallest / len(pieces), high / len(pieces))
        loudness = loudness * jnp.repeat(jnp.exp(draws), shape[position] // parts).reshape((-1,) + (1,) * (len(shape) - 1 - position))
    return loudness


def bell_draw(own_key, shape, scale, bound, pieces=(), held_as=jnp.bfloat16):
    gain = block_scale(own_key, shape, pieces, -0.22, 0.18) if pieces else 1.0
    array = jax.random.normal(own_key, shape, jnp.float32) * scale * gain
    return jnp.minimum(jnp.maximum(array, -bound), bound).astype(held_as)


def gaussian_with(rng, extent, width, reach, cuts, heavy, kind=jnp.bfloat16):
    entries = width * jax.random.normal(rng, extent, jnp.float32)
    if cuts:
        entries = entries * block_scale(rng, extent, cuts, -0.22, 0.18)
    return jnp.clip(raised(entries, jax.random.fold_in(rng, 3), *heavy), -reach, reach).astype(kind)


def setup_inputs(seed: int = 0) -> dict:
    streams_of = jax.random.split(jax.random.key(seed), 17)
    tokens = bell_draw(streams_of[0], (TOKENS, D), 1.0, 6.0, ((0, 32),))
    positions = draw_positions(jax.random.fold_in(streams_of[16], 71), 0)
    w_query = bell_draw(streams_of[2], (D, HEADS * HD), D ** -0.5, 0.25, ((0, 8),))
    w_key = bell_draw(streams_of[3], (D, HD), D ** -0.5, 0.25, ((0, 8),))
    w_value = bell_draw(streams_of[4], (D, HD), D ** -0.5, 0.25, ((0, 8),))
    w_out = bell_draw(streams_of[5], (HEADS * HD, D), (HEADS * HD) ** -0.5, 0.1875, ((1, 8),))
    w_gate = bell_draw(streams_of[6], (D, FF), D ** -0.5, 0.25, ((0, 8),))
    w_up = bell_draw(streams_of[7], (D, FF), D ** -0.5, 0.25, ((0, 8),))
    w_down = bell_draw(streams_of[8], (FF, D), FF ** -0.5, 0.125, ((1, 8),))
    gain_input = jnp.clip(jax.random.uniform(streams_of[9], (D,), jnp.float32, -0.5, 0.5) * block_scale(streams_of[9], (D,), ((0, 8),), -0.4, 0.0), -0.5, 0.5).astype(jnp.bfloat16)
    gain_attn = jnp.clip(jax.random.uniform(streams_of[10], (D,), jnp.float32, -0.5, 0.5) * block_scale(streams_of[10], (D,), ((0, 8),), -0.4, 0.0), -0.5, 0.5).astype(jnp.bfloat16)
    gain_ffn_in = jnp.clip(jax.random.uniform(streams_of[11], (D,), jnp.float32, -0.5, 0.5) * block_scale(streams_of[11], (D,), ((0, 8),), -0.4, 0.0), -0.5, 0.5).astype(jnp.bfloat16)
    gain_ffn_out = jnp.clip(jax.random.uniform(streams_of[12], (D,), jnp.float32, -0.5, 0.5) * block_scale(streams_of[12], (D,), ((0, 8),), -0.4, 0.0), -0.5, 0.5).astype(jnp.bfloat16)
    gain_query = jnp.clip(jax.random.uniform(streams_of[13], (HD,), jnp.float32, -0.5, 0.5) * block_scale(streams_of[13], (HD,), ((0, 8),), -0.4, 0.0), -0.5, 0.5).astype(jnp.bfloat16)
    gain_key = jnp.clip(jax.random.uniform(streams_of[14], (HD,), jnp.float32, -0.5, 0.5) * block_scale(streams_of[14], (HD,), ((0, 8),), -0.4, 0.0), -0.5, 0.5).astype(jnp.bfloat16)
    cotangent = gaussian_with(streams_of[15], (TOKENS, D), 1.0, 6.0, ((0, 32),), (0, 1, 32, 2.75))
    return dict(tokens=tokens, positions=positions, w_query=w_query, w_key=w_key, w_value=w_value, w_out=w_out, w_gate=w_gate, w_up=w_up, w_down=w_down, gain_input=gain_input, gain_attn=gain_attn, gain_ffn_in=gain_ffn_in, gain_ffn_out=gain_ffn_out, gain_query=gain_query, gain_key=gain_key, cotangent=cotangent)


EPS = 1e-06
ROPE_BASE = 10000.0

@jax.custom_vjp
def low(v):
    return lax.optimization_barrier(v.astype(jnp.bfloat16)).astype(jnp.float32)

@jax.custom_vjp
def low_back(v):
    return v

def low_keep(v):
    return (low(v), None)

def low_pass(kept, grad):
    return (grad,)

def back_keep(v):
    return (v, None)

def back_low(kept, grad):
    return (low(grad),)
low.defvjp(low_keep, low_pass)
low_back.defvjp(back_keep, back_low)

def product(left, right):
    return jnp.dot(left, right, precision=lax.Precision.HIGHEST)

def rms_scale(values, gain_vec):
    mean_sq = lax.optimization_barrier(jnp.mean(values * values, axis=-1, keepdims=True))
    return values * lax.rsqrt(mean_sq + EPS) * (1.0 + gain_vec)

def rotate(values, where_pos):
    half_dim = values.shape[-1] // 2
    freq_vec = jnp.exp(jnp.arange(half_dim, dtype=jnp.float32) * (-math.log(ROPE_BASE) / half_dim))
    angle = where_pos.astype(jnp.float32)[:, None] * freq_vec[None, :]
    cosine = jnp.cos(angle)[:, None, :]
    sine = jnp.sin(angle)[:, None, :]
    first_half = values[..., :half_dim]
    second_half = values[..., half_dim:]
    return jnp.concatenate([first_half * cosine - second_half * sine, second_half * cosine + first_half * sine], axis=-1)

def window_mask(first_row, where_pos):
    query_idx = jnp.arange(QBLOCK, dtype=jnp.int32)[:, None]
    key_idx = jnp.arange(QBLOCK + WINDOW, dtype=jnp.int32)[None, :]
    distance = query_idx + WINDOW - key_idx
    key_global = first_row - WINDOW + key_idx
    return (distance >= 0) & (distance < WINDOW) & (distance <= where_pos[:, None]) & (key_global >= 0)

def attention(queries, key_rows, value_rows, positions):
    pad_rows = jnp.zeros((WINDOW, HD), jnp.float32)
    key_ext = jnp.concatenate([pad_rows, key_rows], axis=0)
    value_ext = jnp.concatenate([pad_rows, value_rows], axis=0)

    def one_block(block_idx):
        row_start = block_idx * QBLOCK
        query_part = lax.dynamic_slice_in_dim(queries, row_start, QBLOCK, 0)
        key_part = lax.dynamic_slice_in_dim(key_ext, row_start, QBLOCK + WINDOW, 0)
        value_part = lax.dynamic_slice_in_dim(value_ext, row_start, QBLOCK + WINDOW, 0)
        pos_part = lax.dynamic_slice_in_dim(positions, row_start, QBLOCK, 0)
        scores = low_back(jnp.einsum('qhd,kd->hqk', query_part, key_part, precision=lax.Precision.HIGHEST))
        scores = jnp.where(window_mask(row_start, pos_part)[None], scores, -1e+30)
        row_max = lax.optimization_barrier(jnp.max(scores, axis=-1, keepdims=True))
        exp_scores = jnp.exp(scores - row_max)
        weights = low(exp_scores / lax.optimization_barrier(jnp.sum(exp_scores, axis=-1, keepdims=True)))
        return jnp.einsum('hqk,kd->qhd', weights, value_part, precision=lax.Precision.HIGHEST)
    blocks = lax.map(jax.checkpoint(one_block), jnp.arange(TOKENS // QBLOCK, dtype=jnp.int32))
    return blocks.reshape(TOKENS, HEADS, HD)

def forward(resid, w_query, w_key, w_value, w_out, w_gate, w_up, w_down, gain_input, gain_attn, gain_ffn_in, gain_ffn_out, gain_query, gain_key, positions):
    hidden_in = low(rms_scale(resid, gain_input))
    query_raw = low_back(product(hidden_in, w_query))
    key_raw = low_back(product(hidden_in, w_key))
    value_raw = product(hidden_in, w_value)
    query_rot = rotate(rms_scale(query_raw.reshape(TOKENS, HEADS, HD), gain_query), positions) * HD ** (-0.5)
    queries = low_back(low(query_rot))
    key_rot = rotate(rms_scale(key_raw.reshape(TOKENS, 1, HD), gain_key), positions)[:, 0]
    key_rows = low_back(low(key_rot))
    value_rows = low_back(low(value_raw))
    context = low_back(low(attention(queries, key_rows, value_rows, positions)))
    branch = low_back(product(context.reshape(TOKENS, HEADS * HD), w_out))
    middle = resid + rms_scale(branch, gain_attn)
    hidden_mid = low(rms_scale(middle, gain_ffn_in))
    gate_pre = low_back(product(hidden_mid, w_gate))
    up_pre = low_back(product(hidden_mid, w_up))
    acted = low(jax.nn.gelu(gate_pre, approximate=True) * up_pre)
    down_out = low_back(product(acted, w_down))
    return middle + rms_scale(down_out, gain_ffn_out)

def reference(tokens, positions, w_query, w_key, w_value, w_out, w_gate, w_up, w_down, gain_input, gain_attn, gain_ffn_in, gain_ffn_out, gain_query, gain_key, cotangent):

    def run(resid, wq_f, wk_f, wv_f, wo_f, wg_f, wu_f, wd_f, gi_f, ga_f, gp_f, go_f, gq_f, gk_f):
        return forward(resid, wq_f, wk_f, wv_f, wo_f, wg_f, wu_f, wd_f, gi_f, ga_f, gp_f, go_f, gq_f, gk_f, positions)
    block_out, pull_back = jax.vjp(run, tokens.astype(jnp.float32), w_query.astype(jnp.float32), w_key.astype(jnp.float32), w_value.astype(jnp.float32), w_out.astype(jnp.float32), w_gate.astype(jnp.float32), w_up.astype(jnp.float32), w_down.astype(jnp.float32), gain_input.astype(jnp.float32), gain_attn.astype(jnp.float32), gain_ffn_in.astype(jnp.float32), gain_ffn_out.astype(jnp.float32), gain_query.astype(jnp.float32), gain_key.astype(jnp.float32))
    grads = pull_back(cotangent.astype(jnp.float32))
    return (block_out.astype(jnp.bfloat16), grads[0], grads[1], grads[2], grads[3], grads[4], grads[5], grads[6], grads[7], grads[8], grads[9], grads[10], grads[11], grads[12], grads[13])
```

```python
import math

import jax
import jax.numpy as jnp
from jax import lax
from jax.sharding import PartitionSpec as P

HD = 256
WINDOW = 512
EPS = 1e-06
ROPE_BASE = 10000.0
PAD = 128


def matmul(left, right):
    return jnp.dot(left, right, preferred_element_type=jnp.float32)


def rms_scale(values, gain_vec):
    mean_sq = jnp.mean(values * values, axis=-1, keepdims=True)
    return values * lax.rsqrt(mean_sq + EPS) * (1.0 + gain_vec)


def residual_norm(resid_in, branch_in, gain_vec):
    return resid_in + rms_scale(branch_in, gain_vec)


def geglu(gate_pre, up_pre):
    return jax.nn.gelu(gate_pre, approximate=True) * up_pre


def rope_tables(where_pos):
    half_dim = HD // 2
    freq_vec = jnp.exp(jnp.arange(half_dim, dtype=jnp.float32) * (-math.log(ROPE_BASE) / half_dim))
    angle = where_pos.astype(jnp.float32)[:, None] * freq_vec[None, :]
    return jnp.cos(angle), jnp.sin(angle)


def rotate(values, cosine, sine):
    half_dim = HD // 2
    first_half = values[..., :half_dim]
    second_half = values[..., half_dim:]
    return jnp.concatenate(
        [first_half * cosine - second_half * sine, second_half * cosine + first_half * sine],
        axis=-1,
    )


def bits_of(count):
    return [1 << k for k in range(count.bit_length() - 1)]


def swap(value, axis, bit):
    count = lax.axis_size(axis)
    return lax.ppermute(value, axis, [(i, i ^ bit) for i in range(count)])


def bit_set(axis, bit):
    return (lax.axis_index(axis) & bit) != 0


def gather_steps(shard, axis, order):
    held = []
    buf = shard[None]
    for bit in order:
        recv = swap(buf, axis, bit)
        place = sum(1 for b in held if b > bit)
        held.append(bit)
        lead = 1 << place
        split = (lead, buf.shape[0] // lead) + buf.shape[1:]
        mine, other = buf.reshape(split), recv.reshape(split)
        low = jnp.stack([mine, other], axis=1)
        high = jnp.stack([other, mine], axis=1)
        buf = jnp.where(bit_set(axis, bit), high, low).reshape((-1,) + buf.shape[1:])
        yield buf


def scatter_sum(parts, axis, order):
    left = sorted(order, reverse=True)
    buf = parts
    for bit in order:
        lead = 1 << left.index(bit)
        left.remove(bit)
        shaped = buf.reshape((lead, 2, -1) + buf.shape[1:])
        mine = jnp.where(bit_set(axis, bit), 1, 0)
        send = lax.dynamic_index_in_dim(shaped, 1 - mine, 1, keepdims=False)
        keep = lax.dynamic_index_in_dim(shaped, mine, 1, keepdims=False)
        recv = swap(send, axis, bit)
        buf = (keep.astype(jnp.float32) + recv.astype(jnp.float32)).astype(jnp.bfloat16)
        buf = buf.reshape((-1,) + parts.shape[1:])
    return buf[0]


def sum_whole(value, axis):
    for bit in bits_of(lax.axis_size(axis)):
        recv = swap(value, axis, bit)
        value = (value.astype(jnp.float32) + recv.astype(jnp.float32)).astype(jnp.bfloat16)
    return value


def sum_halved(value, axis):
    bits = bits_of(lax.axis_size(axis))
    for bit in bits:
        half = value.shape[1] // 2
        high = bit_set(axis, bit)
        left, right = value[:, :half], value[:, half:]
        recv = swap(jnp.where(high, left, right), axis, bit)
        keep = jnp.where(high, right, left)
        value = (keep.astype(jnp.float32) + recv.astype(jnp.float32)).astype(jnp.bfloat16)
    for bit in reversed(bits):
        high = bit_set(axis, bit)
        recv = swap(value, axis, bit)
        value = jnp.where(
            high,
            jnp.concatenate([recv, value], axis=1),
            jnp.concatenate([value, recv], axis=1),
        )
    return value


def window_mask(tok_rows, first_row, where_pos):
    query_idx = jnp.arange(tok_rows, dtype=jnp.int32)[:, None]
    key_idx = jnp.arange(tok_rows + WINDOW, dtype=jnp.int32)[None, :]
    distance = query_idx + WINDOW - key_idx
    key_global = first_row - WINDOW + key_idx
    return (
        (distance >= 0) & (distance < WINDOW) & (distance <= where_pos[:, None]) & (key_global >= 0)
    )


def attend_forward(queries, keys, values, pos_rows, first_row):
    scores = jnp.einsum("qhd,kd->hqk", queries, keys, preferred_element_type=jnp.float32)
    allowed = window_mask(queries.shape[0], first_row, pos_rows)[None]
    scores = jnp.where(allowed, scores, -1e30)
    row_max = jnp.max(scores, axis=-1, keepdims=True)
    exp_scores = jnp.exp(scores - row_max)
    row_total = jnp.sum(exp_scores, axis=-1, keepdims=True)
    weights = (exp_scores / row_total).astype(jnp.bfloat16)
    log_total = row_max + jnp.log(row_total)
    context = jnp.einsum("hqk,kd->qhd", weights, values, preferred_element_type=jnp.float32)
    return context.astype(jnp.bfloat16), log_total


def attend_backward(queries, keys, values, pos_rows, first_row, log_total, context_grad):
    scores = jnp.einsum("qhd,kd->hqk", queries, keys, preferred_element_type=jnp.float32)
    allowed = window_mask(queries.shape[0], first_row, pos_rows)[None]
    weights = jnp.where(allowed, jnp.exp(scores - log_total), 0.0)
    weights_low = weights.astype(jnp.bfloat16)
    value_grad = jnp.einsum(
        "hqk,qhd->kd", weights_low, context_grad, preferred_element_type=jnp.float32
    )
    prob_grad = jnp.einsum("qhd,kd->hqk", context_grad, values, preferred_element_type=jnp.float32)
    centre = jnp.sum(weights * prob_grad, axis=-1, keepdims=True)
    score_grad = (weights * (prob_grad - centre)).astype(jnp.bfloat16)
    query_grad = jnp.einsum("hqk,kd->qhd", score_grad, keys, preferred_element_type=jnp.float32)
    key_grad = jnp.einsum("hqk,qhd->kd", score_grad, queries, preferred_element_type=jnp.float32)
    return query_grad.astype(jnp.bfloat16), key_grad, value_grad


def per_device(
    tokens,
    positions,
    w_query,
    w_key,
    w_value,
    w_out,
    w_gate,
    w_up,
    w_down,
    gain_input,
    gain_attn,
    gain_ffn_in,
    gain_ffn_out,
    gain_query,
    gain_key,
    cotangent,
):
    seq_count = lax.axis_size("seq")
    head_count = lax.axis_size("head")
    head_index = lax.axis_index("head")
    seq_index = lax.axis_index("seq")
    tok_rows = tokens.shape[0]
    shard_rows = w_query.shape[0]
    width = shard_rows * seq_count
    ff = w_gate.shape[1]
    q_cols = w_query.shape[1]
    heads = q_cols // HD
    gain_rows = gain_query.shape[0]
    bf16, f32 = jnp.bfloat16, jnp.float32

    total = seq_count * head_count
    rim_tokens = lax.ppermute(
        tokens[tok_rows - WINDOW :], ("seq", "head"), [(i, i + 1) for i in range(total - 1)]
    )

    rising = bits_of(seq_count)
    order_a = rising
    order_b = rising[:1] + rising[:0:-1]

    def column(gain):
        return jnp.pad(gain, (0, shard_rows - gain.shape[0]))[:, None]

    gains = jnp.concatenate(
        [
            column(g)
            for g in (gain_input, gain_attn, gain_ffn_in, gain_ffn_out, gain_query, gain_key)
        ],
        axis=1,
    )
    gains = jnp.pad(gains, ((0, 0), (0, PAD - gains.shape[1])))
    steps_q = list(gather_steps(w_query, "seq", order_a[::-1]))
    steps_kv = list(
        gather_steps(jnp.concatenate([w_key, w_value, gains], axis=1), "seq", order_b[::-1])
    )
    query_all = steps_q[-1].reshape(width, q_cols)
    kvg_all = steps_kv[-1].reshape(width, 2 * HD + PAD)
    shard_a = jnp.concatenate([w_out.T, w_gate], axis=1)
    shard_b = jnp.concatenate([w_up, w_down.T], axis=1)
    shard_a, shard_b, _, _ = lax.optimization_barrier((shard_a, shard_b, steps_q[-2], steps_kv[-2]))
    all_a = list(gather_steps(shard_a, "seq", order_a[::-1]))[-1].reshape(width, q_cols + ff)
    all_b = list(gather_steps(shard_b, "seq", order_b[::-1]))[-1].reshape(width, 2 * ff)
    kv_w = kvg_all[:, : 2 * HD]
    gain_cols = kvg_all[:, 2 * HD : 2 * HD + 8].astype(f32)
    input_all, attn_all, pre_all, post_all = (gain_cols[:, k] for k in range(4))
    qgain_all, kgain_all = (
        gain_cols[:, k].reshape(seq_count, shard_rows)[:, :gain_rows].reshape(-1) for k in (4, 5)
    )
    out_t, gate_all = all_a[:, :q_cols], all_a[:, q_cols:]
    up_all, down_t = all_b[:, :ff], all_b[:, ff:]

    own_pos = lax.dynamic_slice_in_dim(positions, head_index * tok_rows, tok_rows, 0)
    rim_pos = own_pos[0] - WINDOW + jnp.arange(WINDOW, dtype=jnp.int32)
    ext_cos, ext_sin = rope_tables(jnp.concatenate([rim_pos, own_pos]))
    own_cos, own_sin = ext_cos[WINDOW:], ext_sin[WINDOW:]

    def query_prep(raw_rows, gain_vec):
        shaped = raw_rows.reshape(tok_rows, heads, HD)
        turned = rotate(rms_scale(shaped, gain_vec), own_cos[:, None], own_sin[:, None])
        return turned * HD ** (-0.5)

    def key_prep(raw_rows, gain_vec):
        return rotate(rms_scale(raw_rows, gain_vec), own_cos, own_sin)

    resid = tokens.astype(f32)
    normed_in, pull_input = jax.vjp(rms_scale, resid, input_all)
    hidden_in = normed_in.astype(bf16)
    rim_hidden = rms_scale(rim_tokens.astype(f32), input_all).astype(bf16)
    query_raw = matmul(hidden_in, query_all)
    kv_raw = matmul(hidden_in, kv_w)
    rim_raw = matmul(rim_hidden, kv_w)
    key_raw = kv_raw[:, :HD]
    query_rot, pull_query = jax.vjp(query_prep, query_raw, qgain_all)
    key_rot, pull_key = jax.vjp(key_prep, key_raw, kgain_all)
    rim_key = rotate(rms_scale(rim_raw[:, :HD], kgain_all), ext_cos[:WINDOW], ext_sin[:WINDOW])
    queries = query_rot.astype(bf16)
    keys = jnp.concatenate([rim_key.astype(bf16), key_rot.astype(bf16)], axis=0)
    values = jnp.concatenate([rim_raw[:, HD:].astype(bf16), kv_raw[:, HD:].astype(bf16)], axis=0)
    first_row = (seq_index * head_count + head_index) * tok_rows
    context, log_total = attend_forward(queries, keys, values, own_pos, first_row)
    context_seq = context.reshape(tok_rows, heads * HD)
    branch = jnp.einsum("tc,dc->td", context_seq, out_t, preferred_element_type=f32)
    middle, pull_attn = jax.vjp(residual_norm, resid, branch, attn_all)
    normed_mid, pull_pre = jax.vjp(rms_scale, middle, pre_all)
    hidden_mid = normed_mid.astype(bf16)
    gate_pre = matmul(hidden_mid, gate_all)
    up_pre = matmul(hidden_mid, up_all)
    acted_full, pull_act = jax.vjp(geglu, gate_pre, up_pre)
    acted = acted_full.astype(bf16)
    down_out = jnp.einsum("tf,df->td", acted, down_t, preferred_element_type=f32)
    block_out, pull_post = jax.vjp(residual_norm, middle, down_out, post_all)
    grad_y = cotangent.astype(f32)
    grad_mid_post, grad_down, grad_post = pull_post(grad_y)
    down_low = grad_down.astype(bf16)

    def weight_grad(rows, cols):
        product = jnp.einsum("td,tf->df", rows, cols, preferred_element_type=f32)
        return product.astype(bf16)

    grad_acted = matmul(down_low, down_t)
    grad_gate, grad_up = pull_act(grad_acted)
    gate_low = grad_gate.astype(bf16)
    up_low = grad_up.astype(bf16)
    grad_hmid = jnp.einsum("tf,df->td", gate_low, gate_all, preferred_element_type=f32) + jnp.einsum(
        "tf,df->td", up_low, up_all, preferred_element_type=f32
    )
    part_b = jnp.concatenate(
        [weight_grad(hidden_mid, up_low), weight_grad(down_low, acted)], axis=1
    ).reshape(seq_count, shard_rows, 2 * ff)
    grad_mid_pre, grad_pre = pull_pre(grad_hmid)
    grad_resid_attn, grad_branch, grad_attn = pull_attn(grad_mid_post + grad_mid_pre)
    branch_low = grad_branch.astype(bf16)
    part_a = jnp.concatenate(
        [weight_grad(branch_low, context_seq), weight_grad(hidden_mid, gate_low)], axis=1
    ).reshape(seq_count, shard_rows, q_cols + ff)
    grad_context = matmul(branch_low, out_t).astype(bf16).reshape(tok_rows, heads, HD)
    grad_context, part_a, part_b = lax.optimization_barrier((grad_context, part_a, part_b))

    own_a = sum_halved(scatter_sum(part_a, "seq", order_a), "head").astype(f32)
    own_b = sum_halved(scatter_sum(part_b, "seq", order_b), "head").astype(f32)

    query_back, key_grad, value_grad = attend_backward(
        queries, keys, values, own_pos, first_row, log_total, grad_context
    )
    kv_grad = jnp.concatenate([key_grad, value_grad], axis=1)
    rim_in = lax.ppermute(
        kv_grad[:WINDOW].astype(bf16), ("seq", "head"), [(i + 1, i) for i in range(total - 1)]
    )
    own_kv = kv_grad[WINDOW:]
    tail = own_kv[tok_rows - WINDOW :] + rim_in.astype(f32)
    kv_low = jnp.concatenate([own_kv[: tok_rows - WINDOW], tail], axis=0).astype(bf16)
    value_low = kv_low[:, HD:]
    grad_qraw, grad_qgain = pull_query(query_back.astype(f32))
    grad_kraw, grad_kgain = pull_key(kv_low[:, :HD].astype(f32))
    qraw_low = grad_qraw.astype(bf16)
    kv_raw_low = jnp.concatenate([grad_kraw.astype(bf16), value_low], axis=1)
    grad_hin = jnp.einsum("tc,dc->td", qraw_low, query_all, preferred_element_type=f32) + jnp.einsum(
        "tc,dc->td", kv_raw_low, kv_w, preferred_element_type=f32
    )
    part_q = weight_grad(hidden_in, qraw_low).reshape(seq_count, shard_rows, q_cols)
    grad_resid_in, grad_input = pull_input(grad_hin)
    grad_tokens = grad_resid_attn + grad_resid_in

    def spread(gain_grad):
        shaped = gain_grad.reshape(seq_count, -1)
        shaped = jnp.pad(shaped, ((0, 0), (0, shard_rows - shaped.shape[1])))
        return shaped.reshape(width, 1)

    gain_part = jnp.concatenate(
        [
            spread(g)
            for g in (grad_input, grad_attn, grad_pre, grad_post, grad_qgain, grad_kgain)
        ],
        axis=1,
    )
    gain_part = jnp.pad(gain_part, ((0, 0), (0, PAD - gain_part.shape[1]))).astype(bf16)
    part_kv = jnp.concatenate([weight_grad(hidden_in, kv_raw_low), gain_part], axis=1).reshape(
        seq_count, shard_rows, 2 * HD + PAD
    )
    own_q = sum_whole(scatter_sum(part_q, "seq", order_a), "head").astype(f32)
    own_kvg = sum_whole(scatter_sum(part_kv, "seq", order_b), "head").astype(f32)
    own_gains = own_kvg[:, 2 * HD :]
    return (
        block_out.astype(bf16),
        grad_tokens,
        own_q,
        own_kvg[:, :HD],
        own_kvg[:, HD : 2 * HD],
        own_a[:, :q_cols].T,
        own_a[:, q_cols:],
        own_b[:, :ff],
        own_b[:, ff:].T,
        own_gains[:, 0],
        own_gains[:, 1],
        own_gains[:, 2],
        own_gains[:, 3],
        own_gains[:gain_rows, 4],
        own_gains[:gain_rows, 5],
    )


def solution(mesh):
    in_specs = (
        P(("seq", "head"), None),
        P("seq"),
        P("seq", None),
        P("seq", None),
        P("seq", None),
        P(None, "seq"),
        P("seq", None),
        P("seq", None),
        P(None, "seq"),
        P("seq"),
        P("seq"),
        P("seq"),
        P("seq"),
        P("seq"),
        P("seq"),
        P(("seq", "head"), None),
    )
    out_specs = (
        P(("seq", "head"), None),
        P(("seq", "head"), None),
        P("seq", None),
        P("seq", None),
        P("seq", None),
        P(None, "seq"),
        P("seq", None),
        P("seq", None),
        P(None, "seq"),
        P("seq"),
        P("seq"),
        P("seq"),
        P("seq"),
        P("seq"),
        P("seq"),
    )
    return jax.shard_map(
        per_device, mesh=mesh, in_specs=in_specs, out_specs=out_specs, check_vma=False
    )
```

```python
import functools
import math

import jax
import jax.numpy as jnp
from jax import lax
from jax.experimental import pallas as pl
from jax.experimental.pallas import tpu as pltpu
from jax.sharding import PartitionSpec as P

HD = 256
WINDOW = 512
EPS = 1e-06
ROPE_BASE = 10000.0
PAD = 128


def matmul(left, right):
    return jnp.dot(left, right, preferred_element_type=jnp.float32)


def rms_scale(values, gain_vec):
    mean_sq = jnp.mean(values * values, axis=-1, keepdims=True)
    return values * lax.rsqrt(mean_sq + EPS) * (1.0 + gain_vec)


def residual_norm(resid_in, branch_in, gain_vec):
    return resid_in + rms_scale(branch_in, gain_vec)


def geglu(gate_pre, up_pre):
    return jax.nn.gelu(gate_pre, approximate=True) * up_pre


def rope_tables(where_pos):
    half_dim = HD // 2
    freq_vec = jnp.exp(jnp.arange(half_dim, dtype=jnp.float32) * (-math.log(ROPE_BASE) / half_dim))
    angle = where_pos.astype(jnp.float32)[:, None] * freq_vec[None, :]
    return jnp.cos(angle), jnp.sin(angle)


def rotate(values, cosine, sine):
    half_dim = HD // 2
    first_half = values[..., :half_dim]
    second_half = values[..., half_dim:]
    return jnp.concatenate(
        [first_half * cosine - second_half * sine, second_half * cosine + first_half * sine],
        axis=-1,
    )


def bits_of(count):
    return [1 << k for k in range(count.bit_length() - 1)]


def swap(value, axis, bit):
    count = lax.axis_size(axis)
    return lax.ppermute(value, axis, [(i, i ^ bit) for i in range(count)])


def bit_set(axis, bit):
    return (lax.axis_index(axis) & bit) != 0


def gather_steps(shard, axis, order):
    held = []
    buf = shard[None]
    for bit in order:
        recv = swap(buf, axis, bit)
        place = sum(1 for b in held if b > bit)
        held.append(bit)
        lead = 1 << place
        split = (lead, buf.shape[0] // lead) + buf.shape[1:]
        mine, other = buf.reshape(split), recv.reshape(split)
        low = jnp.stack([mine, other], axis=1)
        high = jnp.stack([other, mine], axis=1)
        buf = jnp.where(bit_set(axis, bit), high, low).reshape((-1,) + buf.shape[1:])
        yield buf


def scatter_sum(parts, axis, order):
    left = sorted(order, reverse=True)
    buf = parts
    for bit in order:
        lead = 1 << left.index(bit)
        left.remove(bit)
        shaped = buf.reshape((lead, 2, -1) + buf.shape[1:])
        mine = jnp.where(bit_set(axis, bit), 1, 0)
        send = lax.dynamic_index_in_dim(shaped, 1 - mine, 1, keepdims=False)
        keep = lax.dynamic_index_in_dim(shaped, mine, 1, keepdims=False)
        recv = swap(send, axis, bit)
        buf = (keep.astype(jnp.float32) + recv.astype(jnp.float32)).astype(jnp.bfloat16)
        buf = buf.reshape((-1,) + parts.shape[1:])
    return buf[0]


def sum_whole(value, axis):
    for bit in bits_of(lax.axis_size(axis)):
        recv = swap(value, axis, bit)
        value = (value.astype(jnp.float32) + recv.astype(jnp.float32)).astype(jnp.bfloat16)
    return value


def sum_halved(value, axis):
    bits = bits_of(lax.axis_size(axis))
    for bit in bits:
        half = value.shape[1] // 2
        high = bit_set(axis, bit)
        left, right = value[:, :half], value[:, half:]
        recv = swap(jnp.where(high, left, right), axis, bit)
        keep = jnp.where(high, right, left)
        value = (keep.astype(jnp.float32) + recv.astype(jnp.float32)).astype(jnp.bfloat16)
    for bit in reversed(bits):
        high = bit_set(axis, bit)
        recv = swap(value, axis, bit)
        value = jnp.where(
            high,
            jnp.concatenate([recv, value], axis=1),
            jnp.concatenate([value, recv], axis=1),
        )
    return value


QB = 128


def stack_heads(block, heads):
    return jnp.concatenate([block[:, h * HD : (h + 1) * HD] for h in range(heads)], axis=0)


def unstack_heads(block, heads):
    return jnp.concatenate([block[h * QB : (h + 1) * QB] for h in range(heads)], axis=1)


def allowed_pairs(limit, heads):
    shape = (heads * QB, QB + WINDOW)
    row = lax.broadcasted_iota(jnp.int32, shape, 0) & (QB - 1)
    distance = row + WINDOW - lax.broadcasted_iota(jnp.int32, shape, 1)
    return (distance >= 0) & (distance <= jnp.concatenate([limit] * heads, axis=0))


def nt_dot(left, right):
    return lax.dot_general(left, right, (((1,), (1,)), ((), ())), preferred_element_type=jnp.float32)


def tn_dot(left, right):
    return lax.dot_general(left, right, (((0,), (0,)), ((), ())), preferred_element_type=jnp.float32)


def forward_kernel(heads, query_ref, key_ref, value_ref, limit_ref, context_ref, log_ref):
    window = pl.ds(pl.multiple_of(pl.program_id(0) * QB, QB), QB + WINDOW)
    scores = nt_dot(stack_heads(query_ref[...], heads), key_ref[window, :])
    scores = jnp.where(allowed_pairs(limit_ref[...], heads), scores, -1e30)
    row_max = jnp.max(scores, axis=-1, keepdims=True)
    exp_scores = jnp.exp(scores - row_max)
    row_total = jnp.sum(exp_scores, axis=-1, keepdims=True)
    weights = (exp_scores * (1.0 / row_total)).astype(jnp.bfloat16)
    context = jnp.dot(weights, value_ref[window, :], preferred_element_type=jnp.float32)
    context_ref[...] = unstack_heads(context.astype(jnp.bfloat16), heads)
    log_ref[...] = jnp.broadcast_to(row_max + jnp.log(row_total), log_ref.shape)


def backward_kernel(
    heads,
    query_ref,
    key_ref,
    value_ref,
    limit_ref,
    log_ref,
    grad_ref,
    query_grad_ref,
    key_grad_ref,
    value_grad_ref,
):
    @pl.when(pl.program_id(0) == 0)
    def _():
        key_grad_ref[...] = jnp.zeros_like(key_grad_ref)
        value_grad_ref[...] = jnp.zeros_like(value_grad_ref)

    window = pl.ds(pl.multiple_of(pl.program_id(0) * QB, QB), QB + WINDOW)
    queries = stack_heads(query_ref[...], heads)
    grads = stack_heads(grad_ref[...], heads)
    keys = key_ref[window, :]
    scores = nt_dot(queries, keys)
    allowed = allowed_pairs(limit_ref[...], heads)
    weights = jnp.where(allowed, jnp.exp(scores - log_ref[:, :1]), 0.0)
    value_grad_ref[window, :] += tn_dot(weights.astype(jnp.bfloat16), grads)
    prob_grad = nt_dot(grads, value_ref[window, :])
    centre = jnp.sum(weights * prob_grad, axis=-1, keepdims=True)
    score_grad = (weights * (prob_grad - centre)).astype(jnp.bfloat16)
    query_grad = jnp.dot(score_grad, keys, preferred_element_type=jnp.float32)
    query_grad_ref[...] = unstack_heads(query_grad.astype(jnp.bfloat16), heads)
    key_grad_ref[window, :] += tn_dot(score_grad, queries)


def attention_specs(tok_rows, cols, heads):
    rows = pl.BlockSpec((QB, cols), lambda b: (b, 0))
    whole = pl.BlockSpec((tok_rows + WINDOW, HD), lambda b: (0, 0))
    limit = pl.BlockSpec((QB, 1), lambda b: (b, 0))
    log = pl.BlockSpec((heads * QB, 128), lambda b: (b, 0))
    return rows, whole, limit, log


def attention_cost(tok_rows, heads, products):
    pairs = tok_rows * heads * (QB + WINDOW)
    return pl.CostEstimate(
        flops=2 * products * pairs * HD, bytes_accessed=8 << 20, transcendentals=pairs
    )


def attend_forward(queries, keys, values, limit):
    tok_rows, cols = queries.shape
    heads = cols // HD
    rows, whole, lim, log = attention_specs(tok_rows, cols, heads)
    return pl.pallas_call(
        functools.partial(forward_kernel, heads),
        grid=(tok_rows // QB,),
        in_specs=[rows, whole, whole, lim],
        out_specs=[rows, log],
        out_shape=[
            jax.ShapeDtypeStruct((tok_rows, cols), jnp.bfloat16),
            jax.ShapeDtypeStruct((tok_rows * heads, 128), jnp.float32),
        ],
        compiler_params=pltpu.CompilerParams(vmem_limit_bytes=40 << 20),
        cost_estimate=attention_cost(tok_rows, heads, 2),
    )(queries, keys, values, limit)


def attend_backward(queries, keys, values, limit, log_total, context_grad):
    tok_rows, cols = queries.shape
    heads = cols // HD
    rows, whole, lim, log = attention_specs(tok_rows, cols, heads)
    return pl.pallas_call(
        functools.partial(backward_kernel, heads),
        grid=(tok_rows // QB,),
        in_specs=[rows, whole, whole, lim, log, rows],
        out_specs=[rows, whole, whole],
        out_shape=[
            jax.ShapeDtypeStruct((tok_rows, cols), jnp.bfloat16),
            jax.ShapeDtypeStruct((tok_rows + WINDOW, HD), jnp.float32),
            jax.ShapeDtypeStruct((tok_rows + WINDOW, HD), jnp.float32),
        ],
        compiler_params=pltpu.CompilerParams(vmem_limit_bytes=40 << 20),
        cost_estimate=attention_cost(tok_rows, heads, 5),
    )(queries, keys, values, limit, log_total, context_grad)


def per_device(
    tokens,
    positions,
    w_query,
    w_key,
    w_value,
    w_out,
    w_gate,
    w_up,
    w_down,
    gain_input,
    gain_attn,
    gain_ffn_in,
    gain_ffn_out,
    gain_query,
    gain_key,
    cotangent,
):
    seq_count = lax.axis_size("seq")
    head_count = lax.axis_size("head")
    head_index = lax.axis_index("head")
    seq_index = lax.axis_index("seq")
    tok_rows = tokens.shape[0]
    shard_rows = w_query.shape[0]
    width = shard_rows * seq_count
    ff = w_gate.shape[1]
    q_cols = w_query.shape[1]
    heads = q_cols // HD
    gain_rows = gain_query.shape[0]
    bf16, f32 = jnp.bfloat16, jnp.float32

    total = seq_count * head_count
    rim_tokens = lax.ppermute(
        tokens[tok_rows - WINDOW :], ("seq", "head"), [(i, i + 1) for i in range(total - 1)]
    )

    rising = bits_of(seq_count)
    order_a = rising
    order_b = rising[:1] + rising[:0:-1]

    def column(gain):
        return jnp.pad(gain, (0, shard_rows - gain.shape[0]))[:, None]

    gains = jnp.concatenate(
        [
            column(g)
            for g in (gain_input, gain_attn, gain_ffn_in, gain_ffn_out, gain_query, gain_key)
        ],
        axis=1,
    )
    gains = jnp.pad(gains, ((0, 0), (0, PAD - gains.shape[1])))
    steps_q = list(gather_steps(w_query, "seq", order_a[::-1]))
    steps_kv = list(
        gather_steps(jnp.concatenate([w_key, w_value, gains], axis=1), "seq", order_b[::-1])
    )
    query_all = steps_q[-1].reshape(width, q_cols)
    kvg_all = steps_kv[-1].reshape(width, 2 * HD + PAD)
    shard_a = jnp.concatenate([w_out.T, w_gate], axis=1)
    shard_b = jnp.concatenate([w_up, w_down.T], axis=1)
    shard_a, shard_b, _, _ = lax.optimization_barrier((shard_a, shard_b, steps_q[-2], steps_kv[-2]))
    all_a = list(gather_steps(shard_a, "seq", order_a[::-1]))[-1].reshape(width, q_cols + ff)
    all_b = list(gather_steps(shard_b, "seq", order_b[::-1]))[-1].reshape(width, 2 * ff)
    kv_w = kvg_all[:, : 2 * HD]
    gain_cols = kvg_all[:, 2 * HD : 2 * HD + 8].astype(f32)
    input_all, attn_all, pre_all, post_all = (gain_cols[:, k] for k in range(4))
    qgain_all, kgain_all = (
        gain_cols[:, k].reshape(seq_count, shard_rows)[:, :gain_rows].reshape(-1) for k in (4, 5)
    )
    out_t, gate_all = all_a[:, :q_cols], all_a[:, q_cols:]
    up_all, down_t = all_b[:, :ff], all_b[:, ff:]

    own_pos = lax.dynamic_slice_in_dim(positions, head_index * tok_rows, tok_rows, 0)
    rim_pos = own_pos[0] - WINDOW + jnp.arange(WINDOW, dtype=jnp.int32)
    ext_cos, ext_sin = rope_tables(jnp.concatenate([rim_pos, own_pos]))
    own_cos, own_sin = ext_cos[WINDOW:], ext_sin[WINDOW:]

    def query_prep(raw_rows, gain_vec):
        shaped = raw_rows.reshape(tok_rows, heads, HD)
        turned = rotate(rms_scale(shaped, gain_vec), own_cos[:, None], own_sin[:, None])
        return turned * HD ** (-0.5)

    def key_prep(raw_rows, gain_vec):
        return rotate(rms_scale(raw_rows, gain_vec), own_cos, own_sin)

    resid = tokens.astype(f32)
    normed_in, pull_input = jax.vjp(rms_scale, resid, input_all)
    hidden_in = normed_in.astype(bf16)
    rim_hidden = rms_scale(rim_tokens.astype(f32), input_all).astype(bf16)
    query_raw = matmul(hidden_in, query_all)
    kv_raw = matmul(hidden_in, kv_w)
    rim_raw = matmul(rim_hidden, kv_w)
    key_raw = kv_raw[:, :HD]
    query_rot, pull_query = jax.vjp(query_prep, query_raw, qgain_all)
    key_rot, pull_key = jax.vjp(key_prep, key_raw, kgain_all)
    rim_key = rotate(rms_scale(rim_raw[:, :HD], kgain_all), ext_cos[:WINDOW], ext_sin[:WINDOW])
    queries = query_rot.astype(bf16).reshape(tok_rows, q_cols)
    keys = jnp.concatenate([rim_key.astype(bf16), key_rot.astype(bf16)], axis=0)
    values = jnp.concatenate([rim_raw[:, HD:].astype(bf16), kv_raw[:, HD:].astype(bf16)], axis=0)
    first_row = (seq_index * head_count + head_index) * tok_rows
    reach = first_row + jnp.arange(tok_rows, dtype=jnp.int32)
    limit = jnp.minimum(jnp.minimum(own_pos, reach), WINDOW - 1)[:, None]
    context_seq, log_total = attend_forward(queries, keys, values, limit)
    branch = jnp.einsum("tc,dc->td", context_seq, out_t, preferred_element_type=f32)
    middle, pull_attn = jax.vjp(residual_norm, resid, branch, attn_all)
    normed_mid, pull_pre = jax.vjp(rms_scale, middle, pre_all)
    hidden_mid = normed_mid.astype(bf16)
    gate_pre = matmul(hidden_mid, gate_all)
    up_pre = matmul(hidden_mid, up_all)
    acted_full, pull_act = jax.vjp(geglu, gate_pre, up_pre)
    acted = acted_full.astype(bf16)
    down_out = jnp.einsum("tf,df->td", acted, down_t, preferred_element_type=f32)
    block_out, pull_post = jax.vjp(residual_norm, middle, down_out, post_all)
    grad_y = cotangent.astype(f32)
    grad_mid_post, grad_down, grad_post = pull_post(grad_y)
    down_low = grad_down.astype(bf16)

    def weight_grad(rows, cols):
        product = jnp.einsum("td,tf->df", rows, cols, preferred_element_type=f32)
        return product.astype(bf16)

    grad_acted = matmul(down_low, down_t)
    grad_gate, grad_up = pull_act(grad_acted)
    gate_low = grad_gate.astype(bf16)
    up_low = grad_up.astype(bf16)
    grad_hmid = jnp.einsum("tf,df->td", gate_low, gate_all, preferred_element_type=f32) + jnp.einsum(
        "tf,df->td", up_low, up_all, preferred_element_type=f32
    )
    part_b = jnp.concatenate(
        [weight_grad(hidden_mid, up_low), weight_grad(down_low, acted)], axis=1
    ).reshape(seq_count, shard_rows, 2 * ff)
    grad_mid_pre, grad_pre = pull_pre(grad_hmid)
    grad_resid_attn, grad_branch, grad_attn = pull_attn(grad_mid_post + grad_mid_pre)
    branch_low = grad_branch.astype(bf16)
    part_a = jnp.concatenate(
        [weight_grad(branch_low, context_seq), weight_grad(hidden_mid, gate_low)], axis=1
    ).reshape(seq_count, shard_rows, q_cols + ff)
    grad_context = matmul(branch_low, out_t).astype(bf16)
    grad_context, part_a, part_b = lax.optimization_barrier((grad_context, part_a, part_b))

    own_a = sum_halved(scatter_sum(part_a, "seq", order_a), "head").astype(f32)
    own_b = sum_halved(scatter_sum(part_b, "seq", order_b), "head").astype(f32)

    query_back, key_grad, value_grad = attend_backward(
        queries, keys, values, limit, log_total, grad_context
    )
    kv_grad = jnp.concatenate([key_grad, value_grad], axis=1)
    rim_in = lax.ppermute(
        kv_grad[:WINDOW].astype(bf16), ("seq", "head"), [(i + 1, i) for i in range(total - 1)]
    )
    own_kv = kv_grad[WINDOW:]
    tail = own_kv[tok_rows - WINDOW :] + rim_in.astype(f32)
    kv_low = jnp.concatenate([own_kv[: tok_rows - WINDOW], tail], axis=0).astype(bf16)
    value_low = kv_low[:, HD:]
    grad_qraw, grad_qgain = pull_query(query_back.reshape(tok_rows, heads, HD).astype(f32))
    grad_kraw, grad_kgain = pull_key(kv_low[:, :HD].astype(f32))
    qraw_low = grad_qraw.astype(bf16)
    kv_raw_low = jnp.concatenate([grad_kraw.astype(bf16), value_low], axis=1)
    grad_hin = jnp.einsum("tc,dc->td", qraw_low, query_all, preferred_element_type=f32) + jnp.einsum(
        "tc,dc->td", kv_raw_low, kv_w, preferred_element_type=f32
    )
    part_q = weight_grad(hidden_in, qraw_low).reshape(seq_count, shard_rows, q_cols)
    grad_resid_in, grad_input = pull_input(grad_hin)
    grad_tokens = grad_resid_attn + grad_resid_in

    def spread(gain_grad):
        shaped = gain_grad.reshape(seq_count, -1)
        shaped = jnp.pad(shaped, ((0, 0), (0, shard_rows - shaped.shape[1])))
        return shaped.reshape(width, 1)

    gain_part = jnp.concatenate(
        [
            spread(g)
            for g in (grad_input, grad_attn, grad_pre, grad_post, grad_qgain, grad_kgain)
        ],
        axis=1,
    )
    gain_part = jnp.pad(gain_part, ((0, 0), (0, PAD - gain_part.shape[1]))).astype(bf16)
    part_kv = jnp.concatenate([weight_grad(hidden_in, kv_raw_low), gain_part], axis=1).reshape(
        seq_count, shard_rows, 2 * HD + PAD
    )
    own_q = sum_whole(scatter_sum(part_q, "seq", order_a), "head").astype(f32)
    own_kvg = sum_whole(scatter_sum(part_kv, "seq", order_b), "head").astype(f32)
    own_gains = own_kvg[:, 2 * HD :]
    return (
        block_out.astype(bf16),
        grad_tokens,
        own_q,
        own_kvg[:, :HD],
        own_kvg[:, HD : 2 * HD],
        own_a[:, :q_cols].T,
        own_a[:, q_cols:],
        own_b[:, :ff],
        own_b[:, ff:].T,
        own_gains[:, 0],
        own_gains[:, 1],
        own_gains[:, 2],
        own_gains[:, 3],
        own_gains[:gain_rows, 4],
        own_gains[:gain_rows, 5],
    )


def solution(mesh):
    in_specs = (
        P(("seq", "head"), None),
        P("seq"),
        P("seq", None),
        P("seq", None),
        P("seq", None),
        P(None, "seq"),
        P("seq", None),
        P("seq", None),
        P(None, "seq"),
        P("seq"),
        P("seq"),
        P("seq"),
        P("seq"),
        P("seq"),
        P("seq"),
        P(("seq", "head"), None),
    )
    out_specs = (
        P(("seq", "head"), None),
        P(("seq", "head"), None),
        P("seq", None),
        P("seq", None),
        P("seq", None),
        P(None, "seq"),
        P("seq", None),
        P("seq", None),
        P(None, "seq"),
        P("seq"),
        P("seq"),
        P("seq"),
        P("seq"),
        P("seq"),
        P("seq"),
    )
    return jax.shard_map(
        per_device, mesh=mesh, in_specs=in_specs, out_specs=out_specs, check_vma=False
    )
```

```python
import functools
import math

import jax
import jax.numpy as jnp
from jax import lax
from jax.experimental import pallas as pl
from jax.experimental.pallas import tpu as pltpu
from jax.sharding import PartitionSpec as P

HD = 256
WINDOW = 512
EPS = 1e-06
ROPE_BASE = 10000.0
PAD = 128


def matmul(left, right):
    return jnp.dot(left, right, preferred_element_type=jnp.float32)


def rms_scale(values, gain_vec):
    mean_sq = jnp.mean(values * values, axis=-1, keepdims=True)
    return values * lax.rsqrt(mean_sq + EPS) * (1.0 + gain_vec)


def residual_norm(resid_in, branch_in, gain_vec):
    return resid_in + rms_scale(branch_in, gain_vec)


def geglu(gate_pre, up_pre):
    return jax.nn.gelu(gate_pre, approximate=True) * up_pre


def rope_tables(where_pos):
    half_dim = HD // 2
    freq_vec = jnp.exp(jnp.arange(half_dim, dtype=jnp.float32) * (-math.log(ROPE_BASE) / half_dim))
    angle = where_pos.astype(jnp.float32)[:, None] * freq_vec[None, :]
    return jnp.cos(angle), jnp.sin(angle)


def rotate(values, cosine, sine):
    half_dim = HD // 2
    first_half = values[..., :half_dim]
    second_half = values[..., half_dim:]
    return jnp.concatenate(
        [first_half * cosine - second_half * sine, second_half * cosine + first_half * sine],
        axis=-1,
    )


def bits_of(count):
    return [1 << k for k in range(count.bit_length() - 1)]


def swap(value, axis, bit):
    count = lax.axis_size(axis)
    return lax.ppermute(value, axis, [(i, i ^ bit) for i in range(count)])


def bit_set(axis, bit):
    return (lax.axis_index(axis) & bit) != 0


def gather_steps(shard, axis, order):
    held = []
    buf = shard[None]
    for bit in order:
        recv = swap(buf, axis, bit)
        place = sum(1 for b in held if b > bit)
        held.append(bit)
        lead = 1 << place
        split = (lead, buf.shape[0] // lead) + buf.shape[1:]
        mine, other = buf.reshape(split), recv.reshape(split)
        low = jnp.stack([mine, other], axis=1)
        high = jnp.stack([other, mine], axis=1)
        buf = jnp.where(bit_set(axis, bit), high, low).reshape((-1,) + buf.shape[1:])
        tied = yield buf
        buf = buf if tied is None else tied


def added(keep, recv):
    return (keep.astype(jnp.float32) + recv.astype(jnp.float32)).astype(jnp.bfloat16)


def reduce_steps(parts, order, halved):
    left = sorted(order, reverse=True)
    shape = parts.shape[1:]
    buf = parts
    for bit in order:
        lead = 1 << left.index(bit)
        left.remove(bit)
        shaped = buf.reshape((lead, 2, -1) + shape)
        mine = jnp.where(bit_set("seq", bit), 1, 0)
        send = lax.dynamic_index_in_dim(shaped, 1 - mine, 1, keepdims=False)
        keep = lax.dynamic_index_in_dim(shaped, mine, 1, keepdims=False)
        buf = yield added(keep, swap(send, "seq", bit)).reshape((-1,) + shape)
    value = buf[0]
    bits = bits_of(lax.axis_size("head"))
    for bit in bits:
        if not halved:
            value = yield added(value, swap(value, "head", bit))
            continue
        half = value.shape[1] // 2
        high = bit_set("head", bit)
        low_part, high_part = value[:, :half], value[:, half:]
        recv = swap(jnp.where(high, low_part, high_part), "head", bit)
        value = yield added(jnp.where(high, high_part, low_part), recv)
    for bit in reversed(bits if halved else []):
        high = bit_set("head", bit)
        recv = swap(value, "head", bit)
        value = yield jnp.where(
            high,
            jnp.concatenate([recv, value], axis=1),
            jnp.concatenate([value, recv], axis=1),
        )


def tie(*arrays):
    return lax.optimization_barrier(arrays)


QB = 128


def stack_heads(block, heads):
    return jnp.concatenate([block[:, h * HD : (h + 1) * HD] for h in range(heads)], axis=0)


def unstack_heads(block, heads):
    return jnp.concatenate([block[h * QB : (h + 1) * QB] for h in range(heads)], axis=1)


def allowed_pairs(limit, heads):
    shape = (heads * QB, QB + WINDOW)
    row = lax.broadcasted_iota(jnp.int32, shape, 0) & (QB - 1)
    distance = row + WINDOW - lax.broadcasted_iota(jnp.int32, shape, 1)
    return (distance >= 0) & (distance <= jnp.concatenate([limit] * heads, axis=0))


def nt_dot(left, right):
    return lax.dot_general(left, right, (((1,), (1,)), ((), ())), preferred_element_type=jnp.float32)


def tn_dot(left, right):
    return lax.dot_general(left, right, (((0,), (0,)), ((), ())), preferred_element_type=jnp.float32)


def forward_kernel(heads, query_ref, key_ref, value_ref, limit_ref, context_ref, log_ref):
    window = pl.ds(pl.multiple_of(pl.program_id(0) * QB, QB), QB + WINDOW)
    scores = nt_dot(stack_heads(query_ref[...], heads), key_ref[window, :])
    scores = jnp.where(allowed_pairs(limit_ref[...], heads), scores, -1e30)
    row_max = jnp.max(scores, axis=-1, keepdims=True)
    exp_scores = jnp.exp(scores - row_max)
    row_total = jnp.sum(exp_scores, axis=-1, keepdims=True)
    weights = (exp_scores * (1.0 / row_total)).astype(jnp.bfloat16)
    context = jnp.dot(weights, value_ref[window, :], preferred_element_type=jnp.float32)
    context_ref[...] = unstack_heads(context.astype(jnp.bfloat16), heads)
    log_ref[...] = jnp.broadcast_to(row_max + jnp.log(row_total), log_ref.shape)


def backward_kernel(
    heads,
    query_ref,
    key_ref,
    value_ref,
    limit_ref,
    log_ref,
    grad_ref,
    query_grad_ref,
    key_grad_ref,
    value_grad_ref,
):
    @pl.when(pl.program_id(0) == 0)
    def _():
        key_grad_ref[...] = jnp.zeros_like(key_grad_ref)
        value_grad_ref[...] = jnp.zeros_like(value_grad_ref)

    window = pl.ds(pl.multiple_of(pl.program_id(0) * QB, QB), QB + WINDOW)
    queries = stack_heads(query_ref[...], heads)
    grads = stack_heads(grad_ref[...], heads)
    keys = key_ref[window, :]
    scores = nt_dot(queries, keys)
    allowed = allowed_pairs(limit_ref[...], heads)
    weights = jnp.where(allowed, jnp.exp(scores - log_ref[:, :1]), 0.0)
    value_grad_ref[window, :] += tn_dot(weights.astype(jnp.bfloat16), grads)
    prob_grad = nt_dot(grads, value_ref[window, :])
    centre = jnp.sum(weights * prob_grad, axis=-1, keepdims=True)
    score_grad = (weights * (prob_grad - centre)).astype(jnp.bfloat16)
    query_grad = jnp.dot(score_grad, keys, preferred_element_type=jnp.float32)
    query_grad_ref[...] = unstack_heads(query_grad.astype(jnp.bfloat16), heads)
    key_grad_ref[window, :] += tn_dot(score_grad, queries)


def attention_specs(tok_rows, cols, heads):
    rows = pl.BlockSpec((QB, cols), lambda b: (b, 0))
    whole = pl.BlockSpec((tok_rows + WINDOW, HD), lambda b: (0, 0))
    limit = pl.BlockSpec((QB, 1), lambda b: (b, 0))
    log = pl.BlockSpec((heads * QB, 128), lambda b: (b, 0))
    return rows, whole, limit, log


def attention_cost(tok_rows, heads, products):
    pairs = tok_rows * heads * (QB + WINDOW)
    return pl.CostEstimate(
        flops=2 * products * pairs * HD, bytes_accessed=8 << 20, transcendentals=pairs
    )


def attend_forward(queries, keys, values, limit):
    tok_rows, cols = queries.shape
    heads = cols // HD
    rows, whole, lim, log = attention_specs(tok_rows, cols, heads)
    return pl.pallas_call(
        functools.partial(forward_kernel, heads),
        grid=(tok_rows // QB,),
        in_specs=[rows, whole, whole, lim],
        out_specs=[rows, log],
        out_shape=[
            jax.ShapeDtypeStruct((tok_rows, cols), jnp.bfloat16),
            jax.ShapeDtypeStruct((tok_rows * heads, 128), jnp.float32),
        ],
        compiler_params=pltpu.CompilerParams(vmem_limit_bytes=40 << 20),
        cost_estimate=attention_cost(tok_rows, heads, 2),
    )(queries, keys, values, limit)


def attend_backward(queries, keys, values, limit, log_total, context_grad):
    tok_rows, cols = queries.shape
    heads = cols // HD
    rows, whole, lim, log = attention_specs(tok_rows, cols, heads)
    return pl.pallas_call(
        functools.partial(backward_kernel, heads),
        grid=(tok_rows // QB,),
        in_specs=[rows, whole, whole, lim, log, rows],
        out_specs=[rows, whole, whole],
        out_shape=[
            jax.ShapeDtypeStruct((tok_rows, cols), jnp.bfloat16),
            jax.ShapeDtypeStruct((tok_rows + WINDOW, HD), jnp.float32),
            jax.ShapeDtypeStruct((tok_rows + WINDOW, HD), jnp.float32),
        ],
        compiler_params=pltpu.CompilerParams(vmem_limit_bytes=40 << 20),
        cost_estimate=attention_cost(tok_rows, heads, 5),
    )(queries, keys, values, limit, log_total, context_grad)


def per_device(
    tokens,
    positions,
    w_query,
    w_key,
    w_value,
    w_out,
    w_gate,
    w_up,
    w_down,
    gain_input,
    gain_attn,
    gain_ffn_in,
    gain_ffn_out,
    gain_query,
    gain_key,
    cotangent,
):
    seq_count = lax.axis_size("seq")
    head_count = lax.axis_size("head")
    head_index = lax.axis_index("head")
    seq_index = lax.axis_index("seq")
    tok_rows = tokens.shape[0]
    shard_rows = w_query.shape[0]
    width = shard_rows * seq_count
    ff = w_gate.shape[1]
    q_cols = w_query.shape[1]
    heads = q_cols // HD
    gain_rows = gain_query.shape[0]
    bf16, f32 = jnp.bfloat16, jnp.float32

    total = seq_count * head_count
    rim_tokens = lax.ppermute(
        tokens[tok_rows - WINDOW :], ("seq", "head"), [(i, i + 1) for i in range(total - 1)]
    )

    rising = bits_of(seq_count)
    order_a = rising
    order_b = rising[:1] + rising[:0:-1]

    def column(gain):
        return jnp.pad(gain, (0, shard_rows - gain.shape[0]))[:, None]

    gains = jnp.concatenate(
        [
            column(g)
            for g in (gain_input, gain_attn, gain_ffn_in, gain_ffn_out, gain_query, gain_key)
        ],
        axis=1,
    )
    gains = jnp.pad(gains, ((0, 0), (0, PAD - gains.shape[1])))
    steps_q = list(gather_steps(w_query, "seq", order_a[::-1]))
    steps_kv = list(
        gather_steps(jnp.concatenate([w_key, w_value, gains], axis=1), "seq", order_b[::-1])
    )
    query_all = steps_q[-1].reshape(width, q_cols)
    kvg_all = steps_kv[-1].reshape(width, 2 * HD + PAD)
    shard_a = jnp.concatenate([w_out.T, w_gate], axis=1)
    shard_b = jnp.concatenate([w_up, w_down.T], axis=1)
    shard_a, shard_b, _, _ = lax.optimization_barrier((shard_a, shard_b, steps_q[-2], steps_kv[-2]))
    all_a = list(gather_steps(shard_a, "seq", order_a[::-1]))[-1].reshape(width, q_cols + ff)
    steps_b = gather_steps(shard_b, "seq", order_b[::-1])
    for _ in order_b[:-1]:
        half_b = next(steps_b)
    kv_w = kvg_all[:, : 2 * HD]
    gain_cols = kvg_all[:, 2 * HD : 2 * HD + 8].astype(f32)
    input_all, attn_all, pre_all, post_all = (gain_cols[:, k] for k in range(4))
    qgain_all, kgain_all = (
        gain_cols[:, k].reshape(seq_count, shard_rows)[:, :gain_rows].reshape(-1) for k in (4, 5)
    )
    out_t, gate_all = all_a[:, :q_cols], all_a[:, q_cols:]

    own_pos = lax.dynamic_slice_in_dim(positions, head_index * tok_rows, tok_rows, 0)
    rim_pos = own_pos[0] - WINDOW + jnp.arange(WINDOW, dtype=jnp.int32)
    ext_cos, ext_sin = rope_tables(jnp.concatenate([rim_pos, own_pos]))
    own_cos, own_sin = ext_cos[WINDOW:], ext_sin[WINDOW:]

    def query_prep(raw_rows, gain_vec):
        shaped = raw_rows.reshape(tok_rows, heads, HD)
        turned = rotate(rms_scale(shaped, gain_vec), own_cos[:, None], own_sin[:, None])
        return turned * HD ** (-0.5)

    def key_prep(raw_rows, gain_vec):
        return rotate(rms_scale(raw_rows, gain_vec), own_cos, own_sin)

    resid = tokens.astype(f32)
    normed_in, pull_input = jax.vjp(rms_scale, resid, input_all)
    hidden_in = normed_in.astype(bf16)
    rim_hidden = rms_scale(rim_tokens.astype(f32), input_all).astype(bf16)
    query_raw = matmul(hidden_in, query_all)
    kv_raw = matmul(hidden_in, kv_w)
    rim_raw = matmul(rim_hidden, kv_w)
    key_raw = kv_raw[:, :HD]
    query_rot, pull_query = jax.vjp(query_prep, query_raw, qgain_all)
    key_rot, pull_key = jax.vjp(key_prep, key_raw, kgain_all)
    rim_key = rotate(rms_scale(rim_raw[:, :HD], kgain_all), ext_cos[:WINDOW], ext_sin[:WINDOW])
    queries = query_rot.astype(bf16).reshape(tok_rows, q_cols)
    keys = jnp.concatenate([rim_key.astype(bf16), key_rot.astype(bf16)], axis=0)
    values = jnp.concatenate([rim_raw[:, HD:].astype(bf16), kv_raw[:, HD:].astype(bf16)], axis=0)
    first_row = (seq_index * head_count + head_index) * tok_rows
    reach = first_row + jnp.arange(tok_rows, dtype=jnp.int32)
    limit = jnp.minimum(jnp.minimum(own_pos, reach), WINDOW - 1)[:, None]
    context_seq, log_total = attend_forward(queries, keys, values, limit)
    context_seq, half_b = tie(context_seq, half_b)
    all_b = steps_b.send(half_b).reshape(width, 2 * ff)
    up_all, down_t = all_b[:, :ff], all_b[:, ff:]
    branch = jnp.einsum("tc,dc->td", context_seq, out_t, preferred_element_type=f32)
    middle, pull_attn = jax.vjp(residual_norm, resid, branch, attn_all)
    normed_mid, pull_pre = jax.vjp(rms_scale, middle, pre_all)
    hidden_mid = normed_mid.astype(bf16)
    gate_pre = matmul(hidden_mid, gate_all)
    up_pre = matmul(hidden_mid, up_all)
    acted_full, pull_act = jax.vjp(geglu, gate_pre, up_pre)
    acted = acted_full.astype(bf16)
    down_out = jnp.einsum("tf,df->td", acted, down_t, preferred_element_type=f32)
    block_out, pull_post = jax.vjp(residual_norm, middle, down_out, post_all)
    grad_y = cotangent.astype(f32)
    grad_mid_post, grad_down, grad_post = pull_post(grad_y)
    down_low = grad_down.astype(bf16)

    def weight_grad(rows, cols):
        product = jnp.einsum("td,tf->df", rows, cols, preferred_element_type=f32)
        return product.astype(bf16)

    grad_acted = matmul(down_low, down_t)
    grad_gate, grad_up = pull_act(grad_acted)
    gate_low = grad_gate.astype(bf16)
    up_low = grad_up.astype(bf16)
    grad_hmid = jnp.einsum("tf,df->td", gate_low, gate_all, preferred_element_type=f32) + jnp.einsum(
        "tf,df->td", up_low, up_all, preferred_element_type=f32
    )
    part_b = jnp.concatenate(
        [weight_grad(hidden_mid, up_low), weight_grad(down_low, acted)], axis=1
    ).reshape(seq_count, shard_rows, 2 * ff)
    grad_mid_pre, grad_pre = pull_pre(grad_hmid)
    grad_resid_attn, grad_branch, grad_attn = pull_attn(grad_mid_post + grad_mid_pre)
    branch_low = grad_branch.astype(bf16)
    part_a = jnp.concatenate(
        [weight_grad(branch_low, context_seq), weight_grad(hidden_mid, gate_low)], axis=1
    ).reshape(seq_count, shard_rows, q_cols + ff)
    grad_context = matmul(branch_low, out_t).astype(bf16)
    grad_context, part_a, part_b = lax.optimization_barrier((grad_context, part_a, part_b))

    early = [reduce_steps(part_a, order_a, True), reduce_steps(part_b, order_b, True)]
    early_now = [next(steps) for steps in early]

    query_back, key_grad, value_grad = attend_backward(
        queries, keys, values, limit, log_total, grad_context
    )
    query_back, key_grad, value_grad, *early_now = tie(query_back, key_grad, value_grad, *early_now)
    early_now = [steps.send(value) for steps, value in zip(early, early_now)]
    kv_grad = jnp.concatenate([key_grad, value_grad], axis=1)
    rim_in = lax.ppermute(
        kv_grad[:WINDOW].astype(bf16), ("seq", "head"), [(i + 1, i) for i in range(total - 1)]
    )
    own_kv = kv_grad[WINDOW:]
    tail = own_kv[tok_rows - WINDOW :] + rim_in.astype(f32)
    kv_low = jnp.concatenate([own_kv[: tok_rows - WINDOW], tail], axis=0).astype(bf16)
    value_low = kv_low[:, HD:]
    grad_qraw, grad_qgain = pull_query(query_back.reshape(tok_rows, heads, HD).astype(f32))
    grad_kraw, grad_kgain = pull_key(kv_low[:, :HD].astype(f32))
    qraw_low = grad_qraw.astype(bf16)
    kv_raw_low = jnp.concatenate([grad_kraw.astype(bf16), value_low], axis=1)
    grad_hin = jnp.einsum("tc,dc->td", qraw_low, query_all, preferred_element_type=f32) + jnp.einsum(
        "tc,dc->td", kv_raw_low, kv_w, preferred_element_type=f32
    )
    part_q = weight_grad(hidden_in, qraw_low).reshape(seq_count, shard_rows, q_cols)
    grad_resid_in, grad_input = pull_input(grad_hin)
    grad_tokens = grad_resid_attn + grad_resid_in

    def spread(gain_grad):
        shaped = gain_grad.reshape(seq_count, -1)
        shaped = jnp.pad(shaped, ((0, 0), (0, shard_rows - shaped.shape[1])))
        return shaped.reshape(width, 1)

    gain_part = jnp.concatenate(
        [
            spread(g)
            for g in (grad_input, grad_attn, grad_pre, grad_post, grad_qgain, grad_kgain)
        ],
        axis=1,
    )
    gain_part = jnp.pad(gain_part, ((0, 0), (0, PAD - gain_part.shape[1]))).astype(bf16)
    part_kv = jnp.concatenate([weight_grad(hidden_in, kv_raw_low), gain_part], axis=1).reshape(
        seq_count, shard_rows, 2 * HD + PAD
    )
    late = [reduce_steps(part_q, order_a, False), reduce_steps(part_kv, order_b, False)]
    late_now = [next(steps) for steps in late]
    head_steps = len(bits_of(head_count))
    for _ in range(len(rising) + head_steps - 1):
        early_now, late_now = tie(early_now, late_now)
        early_now = [steps.send(value) for steps, value in zip(early, early_now)]
        late_now = [steps.send(value) for steps, value in zip(late, late_now)]
    for _ in range(len(rising) + 2 * head_steps - 2 - (len(rising) + head_steps - 1)):
        early_now = [steps.send(value) for steps, value in zip(early, early_now)]
    own_a, own_b = (value.astype(f32) for value in early_now)
    own_q, own_kvg = (value.astype(f32) for value in late_now)
    own_gains = own_kvg[:, 2 * HD :]
    return (
        block_out.astype(bf16),
        grad_tokens,
        own_q,
        own_kvg[:, :HD],
        own_kvg[:, HD : 2 * HD],
        own_a[:, :q_cols].T,
        own_a[:, q_cols:],
        own_b[:, :ff],
        own_b[:, ff:].T,
        own_gains[:, 0],
        own_gains[:, 1],
        own_gains[:, 2],
        own_gains[:, 3],
        own_gains[:gain_rows, 4],
        own_gains[:gain_rows, 5],
    )


def solution(mesh):
    in_specs = (
        P(("seq", "head"), None),
        P("seq"),
        P("seq", None),
        P("seq", None),
        P("seq", None),
        P(None, "seq"),
        P("seq", None),
        P("seq", None),
        P(None, "seq"),
        P("seq"),
        P("seq"),
        P("seq"),
        P("seq"),
        P("seq"),
        P("seq"),
        P(("seq", "head"), None),
    )
    out_specs = (
        P(("seq", "head"), None),
        P(("seq", "head"), None),
        P("seq", None),
        P("seq", None),
        P("seq", None),
        P(None, "seq"),
        P("seq", None),
        P("seq", None),
        P(None, "seq"),
        P("seq"),
        P("seq"),
        P("seq"),
        P("seq"),
        P("seq"),
        P("seq"),
    )
    return jax.shard_map(
        per_device, mesh=mesh, in_specs=in_specs, out_specs=out_specs, check_vma=False
    )
```
